32 devices in a mesh: grp: 2 (over y), dev: 4 (over z), tp: 4 (over x, core).
Axes of the slice: x: 2, y: 2, z: 4, core: 2. Of those that a mesh axis runs over, the one named last changes fastest.
Arguments:
- residual_input: bfloat16 [256, 6144], P(('grp', 'dev'), 'tp'), parts along dimension 0, may hold values from -32 to 32
- queries: bfloat16 [256, 6144], P(('grp', 'dev'), 'tp'), parts along dimension 0, may hold values from -6 to 6
- new_kv: bfloat16 [256, 2, 1024], P(('grp', 'dev'), None, 'tp'), parts along dimension 0, may hold values from -6 to 6
- cache: bfloat16 [256, 2, 64, 1024], P(('grp', 'dev'), None, None, 'tp'), parts along dimension 0, may hold values from -6 to 6
- lengths: int32 [256], P(('grp', 'dev')), parts along dimension 0, may hold values from 1 to 64, as said below
- slots: int32 [256], P(('grp', 'dev')), parts along dimension 0, may hold values from 0 to 31, as said below
- out_weight: bfloat16 [6144, 6144], P('tp', 'dev'), may hold values from -0.109375 to 0.109375
- norm_gain: float32 [6144], P('tp'), may hold values from 0.1 to 1.9
- router_weight: bfloat16 [6144, 4], P('tp'), may hold values from -0.078125 to 0.078125
- up_weight: bfloat16 [32768, 6144], P('dev', 'tp'), may hold values from -0.078125 to 0.078125
- down_weight: bfloat16 [32768, 6144], P('dev', 'tp'), may hold values from -0.0625 to 0.0625
- routes: int32 [256, 2], P(('grp', 'dev')), parts along dimension 0, may hold values from 0 to 3, all different within a row; in each aligned block of 32 rows (0 to 31, 32 to 63, ...) at most 24 rows name the same one
Outputs:
- layer_out: bfloat16 [256, 6144], P(('grp', 'dev'), 'tp'), parts along dimension 0
The draws below stay inside these ranges and needn't reach their ends.
There are 2 independent parts, one for each index of `grp`. The reference program is written for one: setup_inputs(seed, part) draws one part's arguments, and reference() takes and returns one part's arrays. A program takes and returns all parts, laid end to end along the dimension named above; an argument that names none is the same for every part. Nothing has to cross between parts.
Inputs may be any that keep to these rules, and one draw needn't show every extreme that they name: `routes`: each row names two different experts; among the 32 rows of one index of dev no expert is named by more than 24 rows. `lengths`: each index of dev has a slot with all 64 positions valid. `slots`: each aligned block of 32 rows (the rows of one index of dev) names every slot 0 to 31 once.
All inputs are finite; a program needn't handle non-finite values.
Results may differ from the reference program's by a relative error of at most 0.005.
Values may be sent and summed in bfloat16 or wider, within the bound.
A program may use at most 128 MiB of HBM per device.

```python
import math
import jax
import jax.numpy as jnp
import numpy as np
from jax import lax

D = 6144
HEADS = 48
KEY_VALUE_HEADS = 8
HEAD_DIM = 128
FF = 8192
EXPERTS = 4
B_DEV = 32
LEN = 64
CAP = 24
ROWS = 128
N_DEV = 4


def draw_queries(key, part):
    key = jax.random.fold_in(key, 1)
    base = jnp.clip(jax.random.normal(key, (ROWS, HEADS * HEAD_DIM), jnp.float32), -6.0, 6.0)
    return base.astype(jnp.bfloat16)


def draw_new_kv(key, part):
    key = jax.random.fold_in(key, 2)
    base = jnp.clip(jax.random.normal(key, (ROWS, 2, KEY_VALUE_HEADS * HEAD_DIM), jnp.float32), -6.0, 6.0)
    return base.astype(jnp.bfloat16)


def draw_cache(key, part):
    key = jax.random.fold_in(key, 3)
    base = jnp.clip(jax.random.normal(key, (ROWS, 2, LEN, KEY_VALUE_HEADS * HEAD_DIM), jnp.float32), -6.0, 6.0)
    return base.astype(jnp.bfloat16)


def draw_residual_input(key, part):
    key = jax.random.fold_in(key, 4)
    column = jnp.arange(D, dtype=jnp.float32)
    rising = jnp.sqrt(1.0 + 2.5 * column / D)
    base = jnp.clip(jax.random.normal(key, (ROWS, D), jnp.float32), -6.0, 6.0) * rising[None, :]
    return base.astype(jnp.bfloat16)


def draw_lengths(key, part):
    key = jax.random.fold_in(key, 5)
    drawn = jax.random.randint(key, (ROWS,), 1, LEN + 1)
    pick = jax.random.randint(jax.random.fold_in(key, 1), (ROWS // B_DEV,), 0, B_DEV)
    longest = jnp.arange(ROWS, dtype=jnp.int32) % B_DEV == jnp.repeat(pick, B_DEV)
    return jnp.where(longest, LEN, drawn).astype(jnp.int32)


def one_block(block_key):
    return jax.random.permutation(block_key, B_DEV)


def draw_slots(key, part):
    key = jax.random.fold_in(key, 6)
    block_keys = jax.random.split(key, ROWS // B_DEV)
    return jax.vmap(one_block)(block_keys).reshape(ROWS).astype(jnp.int32)


def strengthened(result, own_key, source, target, parts, factor):
    def block_of(axis_at):
        return (jnp.arange(result.shape[axis_at]) // (result.shape[axis_at] // parts)).reshape((-1,) + (1,) * (result.ndim - 1 - axis_at))

    one_side = jax.random.permutation(own_key, parts)[block_of(target)]
    far = (block_of(target) + parts // 2) % parts
    return jnp.where((block_of(source) == one_side) | (block_of(source) == far), factor * result, result)


def shard_levels(key, dims, cuts, least, top_value):
    factor_of, own = 1.0, jax.random.fold_in(key, 6)
    for dim, parts in cuts:
        steps = jnp.exp(jax.random.uniform(jax.random.fold_in(own, dim), (parts,), jnp.float32, least / len(cuts), top_value / len(cuts)))
        factor_of = factor_of * jnp.repeat(steps, dims[dim] // parts).reshape([-1 if axis == dim else 1 for axis in range(len(dims))])
    return factor_of


def shared_out(key, own, number, rows, amount, top, most, slope):
    ranking = jax.random.permutation(key, amount)
    packed, ordinary = load_shares(amount, rows * top, most, slope, True), load_shares(amount, rows * top, most, slope, False)
    places = jnp.arange(amount)

    def named(sizes, rotation):
        used = int((sizes > 0).sum())
        fixed = max(1, used // 4)
        passed = fixed + (places - fixed + rotation * (used - fixed)) % max(1, amount - fixed)
        return jnp.zeros((amount,), jnp.int32).at[ranking[jnp.where(places < fixed, places, passed)]].set(jnp.asarray(sizes, jnp.int32))

    sizes = jnp.where(number % 4 == 0, named(packed, number // 4), named(ordinary, number - number // 4 - 1))
    mixed = jax.random.permutation(jax.random.fold_in(own, 3), amount)
    donor, sink = mixed[0:amount // 2 * 2:2], mixed[1:amount // 2 * 2:2]
    slack = jnp.minimum(sizes[donor] - 1, most - sizes[sink]) // 2
    slack = jnp.where((donor == ranking[0]) | (sink == ranking[0]) | (sizes[sink] == 0), 0, jnp.maximum(slack, 0))
    passed = jax.random.randint(jax.random.fold_in(own, 4), (amount // 2,), 0, 1 << 20) % (slack + 1)
    sizes = sizes.at[donor].add(-passed).at[sink].add(passed)
    members = jnp.searchsorted(jnp.cumsum(sizes), jnp.arange(rows * top), side="right").astype(jnp.int32)
    grid = members.reshape(top, rows).T
    grid = grid[jax.random.permutation(jax.random.fold_in(own, 1), rows)]
    rotation = jax.random.randint(jax.random.fold_in(own, 2), (rows, 1), 0, top)
    return jnp.take_along_axis(grid, (jnp.arange(top)[None, :] + rotation) % top, axis=1)


def load_shares(amount, total, reach, lean, full):
    loads = [(1 << 20) // math.isqrt(standing ** lean) + 1 for standing in range(1, amount + 1)]
    largest = reach if full else min(reach, max(-(-total // amount), total * loads[0] // sum(loads)))
    least = 1 if total - largest >= amount - 1 else 0
    holding, rest = [largest] + [least] * (amount - 1), total - largest - least * (amount - 1)
    while rest > 0:
        movable = [i for i in range(1, amount) if holding[i] < largest] or [i for i in range(1, amount) if holding[i] < reach]
        pool, left = sum([loads[i] for i in movable]), rest
        for i in movable:
            more = min(reach - holding[i], max(1, left * loads[i] // pool), rest)
            holding[i] = holding[i] + more
            rest = rest - more
    return np.array(holding)


def gaussian(stream_key, dims, scale, reach, shards=(), kind=jnp.bfloat16):
    values = scale * jax.random.normal(stream_key, dims, jnp.float32)
    if shards:
        values = values * shard_levels(stream_key, dims, shards, -0.22, 0.18)
    return jnp.clip(values, -reach, reach).astype(kind)


def bell_draw_with(rng, extent, deviation, most, shards, heavy, held_as=jnp.bfloat16):
    values = deviation * jax.random.normal(rng, extent, jnp.float32)
    if shards:
        values = values * shard_levels(rng, extent, shards, -0.22, 0.18)
    return jnp.clip(strengthened(values, jax.random.fold_in(rng, 3), *heavy), -most, most).astype(held_as)


def setup_inputs(seed: int = 0, part: int = 0) -> dict:
    arg_keys = jax.random.split(jax.random.key(seed), 13)
    own_keys = jax.random.split(jax.random.fold_in(arg_keys[12], part), 13)
    residual_input = draw_residual_input(jax.random.fold_in(jax.random.fold_in(arg_keys[12], part), 71), part)
    queries = draw_queries(jax.random.fold_in(jax.random.fold_in(arg_keys[12], part), 71), part)
    new_kv = draw_new_kv(jax.random.fold_in(jax.random.fold_in(arg_keys[12], part), 71), part)
    cache = draw_cache(jax.random.fold_in(jax.random.fold_in(arg_keys[12], part), 71), part)
    lengths = draw_lengths(jax.random.fold_in(jax.random.fold_in(arg_keys[12], part), 71), part)
    slots = draw_slots(jax.random.fold_in(jax.random.fold_in(arg_keys[12], part), 71), part)
    out_weight = bell_draw_with(arg_keys[6], (HEADS * HEAD_DIM, D), (HEADS * HEAD_DIM) ** -0.5, 0.109375, ((0, 4), (1, 4)), (0, 1, 4, 2.0))
    norm_gain = jnp.clip(1.0 + 0.18 * jax.random.normal(arg_keys[7], (D,), jnp.float32), 0.1, 1.9)
    router_weight = gaussian(arg_keys[8], (D, EXPERTS), D ** -0.5, 0.078125, ((0, 4),))
    up_weight = gaussian(arg_keys[9], (EXPERTS * FF, D), D ** -0.5, 0.078125, ((0, 4), (1, 4)))
    down_weight = gaussian(arg_keys[10], (EXPERTS * FF, D), FF ** -0.5, 0.0625, ((0, 4), (1, 4)))
    routes_keys = jax.random.split(jax.random.fold_in(own_keys[11], 1), ROWS // B_DEV)
    routes_turns = jax.random.permutation(jax.random.fold_in(own_keys[11], 3), ROWS // B_DEV)
    routes = jax.vmap(lambda own, number: shared_out(jax.random.fold_in(own_keys[11], 2), own, number, B_DEV, EXPERTS, 2, CAP, 2))(routes_keys, routes_turns).reshape((ROWS, 2))
    return dict(residual_input=residual_input, queries=queries, new_kv=new_kv, cache=cache, lengths=lengths, slots=slots, out_weight=out_weight, norm_gain=norm_gain, router_weight=router_weight, up_weight=up_weight, down_weight=down_weight, routes=routes)


eps = 1e-05

def reference(residual_input, queries, new_kv, cache, lengths, slots, out_weight, norm_gain, router_weight, up_weight, down_weight, routes):
    group = HEADS // KEY_VALUE_HEADS
    row_index = jnp.arange(ROWS, dtype=jnp.int32)
    slot_row = (row_index // B_DEV * B_DEV + slots).astype(jnp.int32)
    keys = cache[slot_row, 0].astype(jnp.float32).reshape(ROWS, LEN, KEY_VALUE_HEADS, HEAD_DIM)
    values = cache[slot_row, 1].astype(jnp.float32).reshape(ROWS, LEN, KEY_VALUE_HEADS, HEAD_DIM)
    valid = lengths[slot_row]
    query_vector = queries.astype(jnp.float32).reshape(ROWS, KEY_VALUE_HEADS, group, HEAD_DIM)
    current_key = new_kv[:, 0].astype(jnp.float32).reshape(ROWS, KEY_VALUE_HEADS, HEAD_DIM)
    own_value = new_kv[:, 1].astype(jnp.float32).reshape(ROWS, KEY_VALUE_HEADS, HEAD_DIM)
    scale = HEAD_DIM ** (-0.5)
    scores = jnp.einsum('rkgd,rlkd->rkgl', query_vector, keys, precision=lax.Precision.HIGHEST) * scale
    own = jnp.einsum('rkgd,rkd->rkg', query_vector, current_key, precision=lax.Precision.HIGHEST) * scale
    mask = jnp.arange(LEN, dtype=jnp.int32)[None, None, None, :] < valid[:, None, None, None]
    scores = jnp.where(mask, scores, -jnp.inf)
    top = jnp.maximum(lax.optimization_barrier(jnp.max(scores, -1)), own)
    raised = jnp.exp(scores - top[..., None])
    own_raised = jnp.exp(own - top)
    total = lax.optimization_barrier(jnp.sum(raised, -1)) + own_raised
    probs = (raised / total[..., None]).astype(jnp.bfloat16)
    own_prob = (own_raised / total).astype(jnp.bfloat16)
    attended = jnp.einsum('rkgl,rlkd->rkgd', probs.astype(jnp.float32), values, precision=lax.Precision.HIGHEST)
    attended = attended + own_prob.astype(jnp.float32)[..., None] * own_value[:, :, None, :]
    attention = attended.reshape(ROWS, HEADS * HEAD_DIM).astype(jnp.bfloat16)
    mixed = residual_input.astype(jnp.float32) + jnp.dot(attention, out_weight, preferred_element_type=jnp.float32)
    scale_row = lax.rsqrt(lax.optimization_barrier(jnp.mean(mixed * mixed, 1)) + eps)
    gained = mixed * norm_gain
    normed = (gained * scale_row[:, None]).astype(jnp.bfloat16)
    logits = scale_row[:, None] * jnp.dot(gained, router_weight.astype(jnp.float32), precision=lax.Precision.HIGHEST)
    chosen = jnp.take_along_axis(logits, routes, 1)
    gates = 1.0 / (1.0 + jnp.exp(chosen[:, ::-1] - chosen))
    expert_ids = jnp.arange(EXPERTS, dtype=jnp.int32)[None, None, :]
    coeff = lax.optimization_barrier(jnp.sum(jnp.where(routes[:, :, None] == expert_ids, gates[:, :, None], 0.0), 1))
    pieces = N_DEV // EXPERTS
    width = FF // pieces

    def per_expert(total_out, expert):
        up_rows = lax.dynamic_slice_in_dim(up_weight, (expert * FF).astype(jnp.int32), FF, 0)
        down_rows = lax.dynamic_slice_in_dim(down_weight, (expert * FF).astype(jnp.int32), FF, 0)
        pre = lax.dot_general(normed, up_rows, (((1,), (1,)), ((), ())), preferred_element_type=jnp.float32)
        hidden = jax.nn.silu(pre).astype(jnp.bfloat16)

        def add_piece(index, acc):
            start = (index * width).astype(jnp.int32)
            hidden_tile_block = lax.dynamic_slice_in_dim(hidden, start, width, 1)
            weight_block = lax.dynamic_slice_in_dim(down_rows, start, width, 0)
            part = lax.optimization_barrier(jnp.dot(hidden_tile_block, weight_block, preferred_element_type=jnp.float32).astype(jnp.bfloat16))
            return acc + part.astype(jnp.float32)
        expert_out = lax.fori_loop(0, pieces, add_piece, jnp.zeros((ROWS, D), jnp.float32))
        weight_e = lax.optimization_barrier(jnp.sum(jnp.where(jnp.arange(EXPERTS, dtype=jnp.int32)[None, :] == expert, coeff, 0.0), 1))
        return (total_out + weight_e[:, None] * expert_out, None)
    moe, unused = lax.scan(per_expert, jnp.zeros((ROWS, D), jnp.float32), jnp.arange(EXPERTS, dtype=jnp.int32))
    return (mixed + moe).astype(jnp.bfloat16)
```

```python
import jax
import jax.numpy as jnp
from jax import lax
from jax.experimental import pallas as pl
from jax.experimental.pallas import tpu as pltpu
from jax.sharding import PartitionSpec as P

D = 6144
HEAD_DIM = 128
CAP = 24


eps = 1e-05


MESH = pl.DeviceIdType.MESH
CHUNKS = 8
NT = (((1,), (1,)), ((), ()))


def send(source, target, send_sem, recv_sem, where):
    return pltpu.make_async_remote_copy(
        src_ref=source,
        dst_ref=target,
        send_sem=send_sem,
        recv_sem=recv_sem,
        device_id=where,
        device_id_type=MESH,
    )


def fold(block):
    half = block.shape[1] // 2
    return jnp.concatenate([block[:, :half], block[:, half:]], 0).astype(jnp.bfloat16)


def unfold(block):
    rows = block.shape[0] // 2
    wide = block.astype(jnp.float32)
    return jnp.concatenate([wide[:rows], wide[rows:]], 1)


def layer_kernel(
    att_ref,
    res_ref,
    gain_ref,
    router_ref,
    routes_ref,
    routes_t_ref,
    outw_hbm,
    up_hbm,
    down_hbm,
    out_ref,
    weights,
    outw,
    gathered,
    projected,
    core_out,
    core_in,
    x_out,
    x_in,
    turn_out,
    turn_in,
    mixed_ref,
    stat_out,
    stat_in,
    outgoing,
    arrived,
    flat_ref,
    pair_out,
    pair_in,
    own_pre,
    far_out,
    far_in,
    hid_own,
    hid_in,
    acc,
    back_out,
    back_in,
    weight_sem,
    outw_sem,
    gather_sems,
    hop_sems,
    stat_sems,
    there_sems,
    back_sems,
    pair_sems,
    far_sems,
    hid_sems,
):
    devices, row_count, features = gathered.shape
    slots = weights.shape[0]
    chunk = weights.shape[1]
    half = chunk // 2
    experts = router_ref.shape[0]
    f32 = jnp.float32
    bf16 = jnp.bfloat16
    d = lax.axis_index("dev")
    t = lax.axis_index("tp")
    core = lax.rem(t, 2)
    x = t // 2
    sibling = x * 2 + (1 - core)
    far = (1 - x) * 2 + core

    def up_copy(k):
        return pltpu.make_async_copy(
            up_hbm.at[pl.ds(k * chunk, chunk)], weights.at[k], weight_sem.at[k]
        )

    def down_copy(k):
        return pltpu.make_async_copy(
            down_hbm.at[pl.ds(k * chunk, chunk)],
            weights.at[lax.rem(k + CHUNKS, slots)],
            weight_sem.at[k + CHUNKS],
        )

    outw_copy = pltpu.make_async_copy(outw_hbm, outw, outw_sem)
    outw_copy.start()
    for k in range(CHUNKS):
        up_copy(k).start()
    for k in range(slots - CHUNKS):
        down_copy(k).start()

    barrier = pltpu.get_barrier_semaphore()
    for off in range(1, 4):
        pl.semaphore_signal(
            barrier, inc=1, device_id={"dev": lax.rem(d + off, 4)}, device_id_type=MESH
        )
        pl.semaphore_signal(
            barrier, inc=1, device_id={"tp": lax.rem(t + off, 4)}, device_id_type=MESH
        )

    @pl.when(d != t)
    def _():
        pl.semaphore_signal(barrier, inc=1, device_id={"dev": t, "tp": d}, device_id_type=MESH)
        pl.semaphore_wait(barrier, 7)

    @pl.when(d == t)
    def _():
        pl.semaphore_wait(barrier, 6)

    copies = []
    for off in range(1, 4):
        copy = send(
            att_ref,
            gathered.at[d],
            gather_sems.at[0, off],
            gather_sems.at[1, off],
            {"dev": lax.rem(d + off, 4)},
        )
        copy.start()
        copies.append(copy)
    gathered[d] = att_ref[...]
    outw_copy.wait()
    for copy in copies:
        copy.wait()

    rows_all = gathered[...].reshape(devices * row_count, features)

    @pl.loop(0, 3)
    def _(j):
        cols = pl.ds(pl.multiple_of(j * 512, 512), 512)
        projected[:, :, cols] = jnp.dot(
            rows_all, outw[:, cols], preferred_element_type=f32
        ).reshape(devices, row_count, 512)

    core_out[0] = projected[1 - core].astype(bf16)
    core_out[1] = projected[3 - core].astype(bf16)
    copy_core = send(core_out, core_in, hop_sems.at[0], hop_sems.at[1], {"tp": sibling})
    copy_core.start()
    copy_core.wait()
    x_out[...] = (projected[far] + core_in[1 - x].astype(f32)).astype(bf16)
    copy_x = send(x_out, x_in, hop_sems.at[2], hop_sems.at[3], {"tp": far})
    copy_x.start()
    own = projected[t] + core_in[x].astype(f32)
    copy_x.wait()
    turn_out[...] = (own + x_in[...].astype(f32)).astype(bf16)

    @pl.when(d != t)
    def _():
        copy_turn = send(
            turn_out, turn_in, hop_sems.at[4], hop_sems.at[5], {"dev": t, "tp": d}
        )
        copy_turn.start()
        copy_turn.wait()

    @pl.when(d == t)
    def _():
        turn_in[...] = turn_out[...]

    mixed = res_ref[...].astype(f32) + turn_in[...].astype(f32)
    mixed_ref[...] = mixed
    gained = mixed * gain_ref[...]
    lane = lax.broadcasted_iota(jnp.int32, (row_count, 128), 1)
    stat = jnp.where(lane == experts, jnp.sum(mixed * mixed, 1, keepdims=True), 0.0)
    router = router_ref[...].astype(f32)
    for e in range(experts):
        stat = jnp.where(
            lane == e, jnp.sum(gained * router[e : e + 1, :], 1, keepdims=True), stat
        )
    stat_out[...] = stat
    copies = []
    for off in range(1, 4):
        copy = send(
            stat_out,
            stat_in.at[off],
            stat_sems.at[0, off],
            stat_sems.at[1, off],
            {"tp": lax.rem(t + off, 4)},
        )
        copy.start()
        copies.append(copy)

    first = routes_ref[:, 0:1]
    second = routes_ref[:, 1:2]
    first_hot = (lane == first).astype(f32)
    second_hot = (lane == second).astype(f32)
    row_i = lax.broadcasted_iota(jnp.int32, (row_count, row_count), 0)
    row_j = lax.broadcasted_iota(jnp.int32, (row_count, row_count), 1)
    place = jnp.dot(
        (row_j < row_i).astype(bf16),
        (first_hot + second_hot).astype(bf16),
        preferred_element_type=f32,
    )
    first_place = jnp.sum(first_hot * place, 1, keepdims=True)
    second_place = jnp.sum(second_hot * place, 1, keepdims=True)
    wide_lane = lax.broadcasted_iota(jnp.int32, (row_count, experts * CAP), 1)
    pick_first = (
        wide_lane.astype(f32) == first.astype(f32) * CAP + first_place
    ).astype(bf16)
    pick_second = (
        wide_lane.astype(f32) == second.astype(f32) * CAP + second_place
    ).astype(bf16)
    across = lax.broadcasted_iota(jnp.int32, (8, row_count), 0)
    member_t = (across == routes_t_ref[0:1, :]).astype(f32) + (
        across == routes_t_ref[1:2, :]
    ).astype(f32)
    place_t = jnp.dot(
        member_t.astype(bf16), (row_i < row_j).astype(bf16), preferred_element_type=f32
    )
    slot = lax.broadcasted_iota(jnp.int32, (CAP, row_count), 0).astype(f32)
    select = jnp.concatenate(
        [
            jnp.where(slot == place_t[e : e + 1, :], member_t[e : e + 1, :], 0.0)
            for e in range(experts)
        ],
        0,
    ).astype(bf16)

    for copy in copies:
        copy.wait()
    stat = stat + stat_in[1] + stat_in[2] + stat_in[3]
    square = jnp.sum(jnp.where(lane == experts, stat, 0.0), 1, keepdims=True)
    scale_row = lax.rsqrt(square / D + eps)
    logits = stat * scale_row
    first_logit = jnp.sum(first_hot * logits, 1, keepdims=True)
    second_logit = jnp.sum(second_hot * logits, 1, keepdims=True)
    first_gate = 1.0 / (1.0 + jnp.exp(second_logit - first_logit))
    second_gate = 1.0 / (1.0 + jnp.exp(first_logit - second_logit))
    normed = (gained * scale_row).astype(bf16)
    picked = jnp.dot(select, normed, preferred_element_type=f32)
    for e in range(experts):
        outgoing[e] = fold(picked[e * CAP : (e + 1) * CAP])
    copies = []
    for off in range(1, 4):
        peer = lax.rem(d + off, 4)
        copy = send(
            outgoing.at[peer],
            arrived.at[d],
            there_sems.at[0, off],
            there_sems.at[1, off],
            {"dev": peer},
        )
        copy.start()
        copies.append(copy)
    arrived[d] = outgoing[d]
    acc[...] = jnp.zeros_like(acc)
    for copy in copies:
        copy.wait()
    flat_ref[...] = jnp.concatenate([unfold(arrived[s]) for s in range(4)], 0).astype(bf16)

    def pair_copy(k):
        return send(
            pair_out.at[k], pair_in.at[k], pair_sems.at[0, k], pair_sems.at[1, k], {"tp": sibling}
        )

    def far_copy(k):
        return send(
            far_out.at[k], far_in.at[k], far_sems.at[0, k], far_sems.at[1, k], {"tp": far}
        )

    def hid_copy(k):
        return send(
            hid_own.at[k], hid_in.at[k], hid_sems.at[0, k], hid_sems.at[1, k], {"tp": sibling}
        )

    mine = pl.ds(pl.multiple_of(core * half, half), half)
    others = pl.ds(pl.multiple_of((1 - core) * half, half), half)

    @pl.loop(0, CHUNKS + 4)
    def _(s):
        @pl.when(s < CHUNKS)
        def _():
            k = s
            up_copy(k).wait()
            pair_out[k] = lax.dot_general(
                flat_ref[...], weights[k, others, :], NT, preferred_element_type=f32
            ).astype(bf16)
            pair_copy(k).start()
            own_pre[k] = lax.dot_general(
                flat_ref[...], weights[k, mine, :], NT, preferred_element_type=f32
            )

            @pl.when(k < 2 * CHUNKS - slots)
            def _():
                down_copy(k + slots - CHUNKS).start()

        @pl.when((s >= 1) & (s < CHUNKS + 1))
        def _():
            k = s - 1
            pair_copy(k).wait()
            both = own_pre[k] + pair_in[k].astype(f32)
            own_pre[k] = both
            far_out[k] = both.astype(bf16)
            far_copy(k).start()

        @pl.when((s >= 3) & (s < CHUNKS + 3))
        def _():
            k = s - 3
            far_copy(k).wait()
            pre = own_pre[k] + far_in[k].astype(f32)
            hid_own[k] = (pre / (1.0 + jnp.exp(-pre))).astype(bf16)
            hid_copy(k).start()

        @pl.when(s >= 4)
        def _():
            k = s - 4
            place_k = lax.rem(k + CHUNKS, slots)
            down_copy(k).wait()
            acc[...] += jnp.dot(
                hid_own[k], weights[place_k, mine, :], preferred_element_type=f32
            )
            hid_copy(k).wait()
            acc[...] += jnp.dot(
                hid_in[k], weights[place_k, others, :], preferred_element_type=f32
            )

    for s in range(4):
        back_out[s] = fold(acc[s * CAP : (s + 1) * CAP, :])
    copies = []
    for off in range(1, 4):
        peer = lax.rem(d + off, 4)
        copy = send(
            back_out.at[peer],
            back_in.at[d],
            back_sems.at[0, off],
            back_sems.at[1, off],
            {"dev": peer},
        )
        copy.start()
        copies.append(copy)
    back_in[d] = back_out[d]
    for copy in copies:
        copy.wait()
    returned = jnp.concatenate([unfold(back_in[s]) for s in range(4)], 0).astype(bf16)
    out_ref[...] = (
        mixed_ref[...]
        + first_gate * jnp.dot(pick_first, returned, preferred_element_type=f32)
        + second_gate * jnp.dot(pick_second, returned, preferred_element_type=f32)
    ).astype(bf16)


def fused_layer(
    attention, residual_input, norm_gain, router_weight, routes, out_weight, up_weight, down_weight
):
    row_count, features = residual_input.shape
    hidden = up_weight.shape[0]
    chunk = hidden // CHUNKS
    half = chunk // 2
    rows = 4 * CAP
    slots = 14
    f32, bf16 = jnp.float32, jnp.bfloat16
    vmem = pl.BlockSpec(memory_space=pltpu.VMEM)
    hbm = pl.BlockSpec(memory_space=pl.ANY)
    dma = pltpu.SemaphoreType.DMA
    folded = (4, 2 * CAP, features // 2)
    block = (row_count, features)
    scratch = [
        pltpu.VMEM((slots, chunk, features), bf16),
        pltpu.VMEM(out_weight.shape, bf16),
        pltpu.VMEM((4,) + block, bf16),
        pltpu.VMEM((4,) + block, f32),
        pltpu.VMEM((2,) + block, bf16),
        pltpu.VMEM((2,) + block, bf16),
        pltpu.VMEM(block, bf16),
        pltpu.VMEM(block, bf16),
        pltpu.VMEM(block, bf16),
        pltpu.VMEM(block, bf16),
        pltpu.VMEM(block, f32),
        pltpu.VMEM((row_count, 128), f32),
        pltpu.VMEM((4, row_count, 128), f32),
        pltpu.VMEM(folded, bf16),
        pltpu.VMEM(folded, bf16),
        pltpu.VMEM((rows, features), bf16),
        pltpu.VMEM((CHUNKS, rows, half), bf16),
        pltpu.VMEM((CHUNKS, rows, half), bf16),
        pltpu.VMEM((CHUNKS, rows, half), f32),
        pltpu.VMEM((CHUNKS, rows, half), bf16),
        pltpu.VMEM((CHUNKS, rows, half), bf16),
        pltpu.VMEM((CHUNKS, rows, half), bf16),
        pltpu.VMEM((CHUNKS, rows, half), bf16),
        pltpu.VMEM((rows, features), f32),
        pltpu.VMEM(folded, bf16),
        pltpu.VMEM(folded, bf16),
        dma((2 * CHUNKS,)),
        dma,
        dma((2, 4)),
        dma((6,)),
        dma((2, 4)),
        dma((2, 4)),
        dma((2, 4)),
        dma((2, CHUNKS)),
        dma((2, CHUNKS)),
        dma((2, CHUNKS)),
    ]
    return pl.pallas_call(
        layer_kernel,
        out_shape=jax.ShapeDtypeStruct(block, bf16),
        in_specs=[vmem] * 6 + [hbm] * 3,
        out_specs=vmem,
        scratch_shapes=scratch,
        compiler_params=pltpu.CompilerParams(
            collective_id=0, has_side_effects=True, vmem_limit_bytes=60 * 1024 * 1024
        ),
        cost_estimate=pl.CostEstimate(
            flops=4 * rows * hidden * features,
            bytes_accessed=4 * hidden * features + out_weight.size * 2,
            transcendentals=rows * hidden,
        ),
    )(
        attention,
        residual_input,
        norm_gain.reshape(1, features),
        router_weight.T,
        routes,
        routes.T,
        out_weight,
        up_weight,
        down_weight,
    )


def sum_heads(terms):
    return lax.psum_scatter(terms, "tp", scatter_dimension=1, tiled=True)


def body(
    residual_input,
    queries,
    new_kv,
    cache,
    lengths,
    slots,
    out_weight,
    norm_gain,
    router_weight,
    up_weight,
    down_weight,
    routes,
):
    row_count = residual_input.shape[0]
    features = residual_input.shape[1]
    kv_local = cache.shape[3] // HEAD_DIM
    group = queries.shape[1] // cache.shape[3]
    positions = cache.shape[2]
    experts = router_weight.shape[1]
    devices = lax.axis_size("dev")
    pieces = devices // experts
    capacity = CAP
    placing = (slots[:, None] == lax.broadcasted_iota(jnp.int32, (row_count, row_count), 1)).astype(
        jnp.bfloat16
    )
    contract_rows = (((0,), (0,)), ((), ()))
    query_slot = lax.dot_general(
        placing, queries, contract_rows, preferred_element_type=jnp.float32
    ).astype(jnp.bfloat16)
    current_slot = lax.dot_general(
        placing, new_kv.reshape(row_count, -1), contract_rows, preferred_element_type=jnp.float32
    ).astype(jnp.bfloat16)
    current_slot = current_slot.reshape(row_count, 2, kv_local, HEAD_DIM)
    query_vector = query_slot.reshape(row_count, kv_local, group, HEAD_DIM)
    keys = cache[:, 0].reshape(row_count, positions, kv_local, HEAD_DIM)
    values = cache[:, 1].reshape(row_count, positions, kv_local, HEAD_DIM)
    scale = HEAD_DIM ** (-0.5)
    scores = (
        jnp.einsum("bkgd,blkd->bkgl", query_vector, keys, preferred_element_type=jnp.float32)
        * scale
    )
    own = (
        jnp.einsum(
            "orwm,orm->orw", query_vector, current_slot[:, 0], preferred_element_type=jnp.float32
        )
        * scale
    )
    mask = lax.broadcasted_iota(jnp.int32, (1, 1, 1, positions), 3) < lengths[:, None, None, None]
    scores = jnp.where(mask, scores, -jnp.inf)
    top = jnp.maximum(jnp.max(scores, -1), own)
    raised = jnp.exp(scores - top[..., None])
    own_raised = jnp.exp(own - top)
    total = jnp.sum(raised, -1) + own_raised
    probs = (raised / total[..., None]).astype(jnp.bfloat16)
    own_prob = (own_raised / total).astype(jnp.bfloat16)
    attended = jnp.einsum("bkgl,blkd->bkgd", probs, values, preferred_element_type=jnp.float32)
    attended = (
        attended
        + own_prob.astype(jnp.float32)[..., None]
        * current_slot[:, 1].astype(jnp.float32)[:, :, None, :]
    )
    attention_slot = attended.reshape(row_count, -1).astype(jnp.bfloat16)
    attention = jnp.dot(placing, attention_slot, preferred_element_type=jnp.float32).astype(
        jnp.bfloat16
    )
    if devices == 4 and lax.axis_size("tp") == 4 and experts == 4:
        return fused_layer(
            attention,
            residual_input,
            norm_gain,
            router_weight,
            routes,
            out_weight,
            up_weight,
            down_weight,
        )
    partial_rows = jnp.dot(
        lax.all_gather(attention, "dev", axis=0, tiled=True),
        out_weight,
        preferred_element_type=jnp.float32,
    )
    terms = lax.all_to_all(partial_rows, "dev", split_axis=0, concat_axis=1, tiled=True)
    projected = sum_heads(terms)
    mixed = residual_input.astype(jnp.float32) + projected
    gained = mixed * norm_gain
    router = router_weight.astype(jnp.float32)
    square = lax.psum(jnp.sum(mixed * mixed, 1), "tp")
    scale_row = lax.rsqrt(square / D + eps)
    normed_wide = gained * scale_row[:, None]
    logits = lax.psum(jnp.dot(normed_wide, router, precision=lax.Precision.HIGHEST), "tp")
    normed = normed_wide.astype(jnp.bfloat16)
    expert_ids = lax.broadcasted_iota(jnp.int32, (row_count, experts), 1)
    first = (routes[:, 0:1] == expert_ids).astype(jnp.float32)
    second = (routes[:, 1:2] == expert_ids).astype(jnp.float32)
    first_logit = jnp.sum(logits * first, 1)
    second_logit = jnp.sum(logits * second, 1)
    first_gate = 1.0 / (1.0 + jnp.exp(second_logit - first_logit))
    second_gate = 1.0 / (1.0 + jnp.exp(first_logit - second_logit))
    row_weight_matrix = first * first_gate[:, None] + second * second_gate[:, None]
    member = first + second
    position = jnp.cumsum(member, 0) - member
    slot_grid = lax.broadcasted_iota(jnp.float32, (1, capacity, 1), 1)
    selection = member.T[:, None, :] * (position.T[:, None, :] == slot_grid).astype(jnp.float32)
    outgoing = jnp.einsum(
        "ecb,bf->ecf", selection.astype(jnp.bfloat16), normed, preferred_element_type=jnp.float32
    ).astype(jnp.bfloat16)
    outgoing = jnp.broadcast_to(outgoing[:, None], (experts, pieces, capacity, features)).reshape(
        devices, capacity, features
    )
    arrived = lax.all_to_all(outgoing, "dev", split_axis=0, concat_axis=0, tiled=True)
    count = arrived.shape[1]
    flat = arrived.reshape(devices * count, features)
    pre = lax.dot_general(
        flat, up_weight, (((1,), (1,)), ((), ())), preferred_element_type=jnp.float32
    )
    summed = lax.psum(pre, "tp")
    hidden = jax.nn.silu(summed).astype(jnp.bfloat16)
    part = jnp.dot(hidden, down_weight, preferred_element_type=jnp.float32).astype(jnp.bfloat16)
    returned = lax.all_to_all(
        part.reshape(devices, count, features), "dev", split_axis=0, concat_axis=0, tiled=True
    )
    expert_sum = jnp.sum(
        returned.reshape(experts, pieces, capacity, features).astype(jnp.float32), 1
    )
    placed = selection * row_weight_matrix.T[:, None, :]
    moe = jnp.einsum("ecb,ecf->bf", placed, expert_sum, precision=lax.Precision.HIGHEST)
    return (mixed + moe).astype(jnp.bfloat16)


def solution(mesh):
    in_specs = (
        P(("grp", "dev"), "tp"),
        P(("grp", "dev"), "tp"),
        P(("grp", "dev"), None, "tp"),
        P(("grp", "dev"), None, None, "tp"),
        P(("grp", "dev")),
        P(("grp", "dev")),
        P("tp", "dev"),
        P("tp"),
        P("tp", None),
        P("dev", "tp"),
        P("dev", "tp"),
        P(("grp", "dev"), None),
    )
    out_specs = P(("grp", "dev"), "tp")
    return jax.shard_map(body, mesh=mesh, in_specs=in_specs, out_specs=out_specs, check_vma=False)
```

```python
import jax
import jax.numpy as jnp
from jax import lax
from jax.experimental import pallas as pl
from jax.experimental.pallas import tpu as pltpu
from jax.sharding import PartitionSpec as P

D = 6144
HEAD_DIM = 128
CAP = 24


eps = 1e-05


MESH = pl.DeviceIdType.MESH
CHUNKS = 8
NT = (((1,), (1,)), ((), ()))


def send(source, target, send_sem, recv_sem, where):
    return pltpu.make_async_remote_copy(
        src_ref=source,
        dst_ref=target,
        send_sem=send_sem,
        recv_sem=recv_sem,
        device_id=where,
        device_id_type=MESH,
    )


def fold(block):
    half = block.shape[1] // 2
    return jnp.concatenate([block[:, :half], block[:, half:]], 0).astype(jnp.bfloat16)


def unfold(block):
    rows = block.shape[0] // 2
    wide = block.astype(jnp.float32)
    return jnp.concatenate([wide[:rows], wide[rows:]], 1)


def layer_kernel(
    att_ref,
    res_ref,
    gain_ref,
    router_ref,
    routes_t_ref,
    outw_hbm,
    up_hbm,
    down_hbm,
    out_ref,
    weights,
    outw,
    gathered,
    projected,
    core_out,
    core_in,
    x_out,
    x_in,
    turn_out,
    turn_in,
    mixed_ref,
    stat_out,
    stat_in,
    outgoing,
    arrived,
    flat_ref,
    pair_out,
    pair_in,
    own_pre,
    far_out,
    far_in,
    hid_own,
    hid_in,
    acc,
    back_out,
    back_in,
    weight_sem,
    outw_sem,
    gather_sems,
    hop_sems,
    stat_sems,
    there_sems,
    back_sems,
    pair_sems,
    far_sems,
    hid_sems,
):
    devices, row_count, features = gathered.shape
    slots = weights.shape[0]
    chunk = weights.shape[1]
    half = chunk // 2
    experts = router_ref.shape[0]
    f32 = jnp.float32
    bf16 = jnp.bfloat16
    d = lax.axis_index("dev")
    t = lax.axis_index("tp")
    core = lax.rem(t, 2)
    x = t // 2
    sibling = x * 2 + (1 - core)
    far = (1 - x) * 2 + core

    def up_copy(k):
        return pltpu.make_async_copy(
            up_hbm.at[pl.ds(k * chunk, chunk)], weights.at[k], weight_sem.at[k]
        )

    def down_copy(k):
        return pltpu.make_async_copy(
            down_hbm.at[pl.ds(k * chunk, chunk)],
            weights.at[lax.rem(k + CHUNKS, slots)],
            weight_sem.at[k + CHUNKS],
        )

    outw_copy = pltpu.make_async_copy(outw_hbm, outw, outw_sem)
    outw_copy.start()
    for k in range(CHUNKS):
        up_copy(k).start()
    for k in range(slots - CHUNKS):
        down_copy(k).start()

    barrier = pltpu.get_barrier_semaphore()
    for off in range(1, 4):
        pl.semaphore_signal(
            barrier, inc=1, device_id={"dev": lax.rem(d + off, 4)}, device_id_type=MESH
        )
        pl.semaphore_signal(
            barrier, inc=1, device_id={"tp": lax.rem(t + off, 4)}, device_id_type=MESH
        )

    @pl.when(d != t)
    def _():
        pl.semaphore_signal(barrier, inc=1, device_id={"dev": t, "tp": d}, device_id_type=MESH)
        pl.semaphore_wait(barrier, 7)

    @pl.when(d == t)
    def _():
        pl.semaphore_wait(barrier, 6)

    copies = []
    for off in range(1, 4):
        copy = send(
            att_ref,
            gathered.at[d],
            gather_sems.at[0, off],
            gather_sems.at[1, off],
            {"dev": lax.rem(d + off, 4)},
        )
        copy.start()
        copies.append(copy)
    gathered[d] = att_ref[...]
    outw_copy.wait()
    for copy in copies:
        copy.wait()

    rows_all = gathered[...].reshape(devices * row_count, features)

    cuts = core_out.shape[0]
    width = features // cuts
    core_copies = []
    for j in range(cuts):
        cols = slice(j * width, (j + 1) * width)
        projected[j] = jnp.dot(
            rows_all, outw[:, cols], preferred_element_type=f32
        ).reshape(devices, row_count, width)
        core_out[j, 0] = projected[j, 1 - core].astype(bf16)
        core_out[j, 1] = projected[j, 3 - core].astype(bf16)
        copy = send(
            core_out.at[j], core_in.at[j], hop_sems.at[0, j], hop_sems.at[1, j], {"tp": sibling}
        )
        copy.start()
        core_copies.append(copy)
    x_copies = []
    for j in range(cuts):
        core_copies[j].wait()
        x_out[j] = (projected[j, far] + core_in[j, 1 - x].astype(f32)).astype(bf16)
        copy = send(x_out.at[j], x_in.at[j], hop_sems.at[2, j], hop_sems.at[3, j], {"tp": far})
        copy.start()
        x_copies.append(copy)

    def turn_copy(j):
        return send(
            turn_out.at[j],
            turn_in.at[j],
            hop_sems.at[4, j],
            hop_sems.at[5, j],
            {"dev": t, "tp": d},
        )

    for j in range(cuts):
        x_copies[j].wait()
        turn_out[j] = (
            projected[j, t] + core_in[j, x].astype(f32) + x_in[j].astype(f32)
        ).astype(bf16)

        @pl.when(d != t)
        def _():
            turn_copy(j).start()

        @pl.when(d == t)
        def _():
            turn_in[j] = turn_out[j]

    @pl.when(d != t)
    def _():
        for j in range(cuts):
            turn_copy(j).wait()

    turned = jnp.concatenate([turn_in[j] for j in range(cuts)], 1)
    mixed = res_ref[...].astype(f32) + turned.astype(f32)
    mixed_ref[...] = mixed
    gain = jnp.concatenate([gain_ref[i : i + 1, :] for i in range(gain_ref.shape[0])], 1)
    gained = mixed * gain
    lane = lax.broadcasted_iota(jnp.int32, (row_count, 128), 1)
    stat = jnp.where(lane == experts, jnp.sum(mixed * mixed, 1, keepdims=True), 0.0)
    router = router_ref[...].astype(f32)
    for e in range(experts):
        stat = jnp.where(
            lane == e, jnp.sum(gained * router[e : e + 1, :], 1, keepdims=True), stat
        )
    stat_out[...] = stat
    copies = []
    for off in range(1, 4):
        copy = send(
            stat_out,
            stat_in.at[off],
            stat_sems.at[0, off],
            stat_sems.at[1, off],
            {"tp": lax.rem(t + off, 4)},
        )
        copy.start()
        copies.append(copy)

    row_i = lax.broadcasted_iota(jnp.int32, (row_count, row_count), 0)
    row_j = lax.broadcasted_iota(jnp.int32, (row_count, row_count), 1)
    same = row_i == row_j
    routes_wide = routes_t_ref[...].astype(f32)
    first = jnp.sum(jnp.where(same, routes_wide[0:1, :], 0.0), 1, keepdims=True)
    second = jnp.sum(jnp.where(same, routes_wide[1:2, :], 0.0), 1, keepdims=True)
    first_hot = (lane.astype(f32) == first).astype(f32)
    second_hot = (lane.astype(f32) == second).astype(f32)
    place = jnp.dot(
        (row_j < row_i).astype(bf16),
        (first_hot + second_hot).astype(bf16),
        preferred_element_type=f32,
    )
    first_place = jnp.sum(first_hot * place, 1, keepdims=True)
    second_place = jnp.sum(second_hot * place, 1, keepdims=True)
    wide_lane = lax.broadcasted_iota(jnp.int32, (row_count, experts * CAP), 1)
    pick_first = (
        wide_lane.astype(f32) == first * CAP + first_place
    ).astype(bf16)
    pick_second = (
        wide_lane.astype(f32) == second * CAP + second_place
    ).astype(bf16)
    across = lax.broadcasted_iota(jnp.int32, (8, row_count), 0)
    member_t = (across == routes_t_ref[0:1, :]).astype(f32) + (
        across == routes_t_ref[1:2, :]
    ).astype(f32)
    place_t = jnp.dot(
        member_t.astype(bf16), (row_i < row_j).astype(bf16), preferred_element_type=f32
    )
    slot = lax.broadcasted_iota(jnp.int32, (CAP, row_count), 0).astype(f32)
    select = jnp.concatenate(
        [
            jnp.where(slot == place_t[e : e + 1, :], member_t[e : e + 1, :], 0.0)
            for e in range(experts)
        ],
        0,
    ).astype(bf16)

    for copy in copies:
        copy.wait()
    stat = stat + stat_in[1] + stat_in[2] + stat_in[3]
    square = jnp.sum(jnp.where(lane == experts, stat, 0.0), 1, keepdims=True)
    scale_row = lax.rsqrt(square / D + eps)
    logits = stat * scale_row
    first_logit = jnp.sum(first_hot * logits, 1, keepdims=True)
    second_logit = jnp.sum(second_hot * logits, 1, keepdims=True)
    first_gate = 1.0 / (1.0 + jnp.exp(second_logit - first_logit))
    second_gate = 1.0 / (1.0 + jnp.exp(first_logit - second_logit))
    normed = (gained * scale_row).astype(bf16)
    picked = jnp.dot(select, normed, preferred_element_type=f32)
    for e in range(experts):
        outgoing[e] = fold(picked[e * CAP : (e + 1) * CAP])
    copies = []
    for off in range(1, 4):
        peer = lax.rem(d + off, 4)
        copy = send(
            outgoing.at[peer],
            arrived.at[d],
            there_sems.at[0, off],
            there_sems.at[1, off],
            {"dev": peer},
        )
        copy.start()
        copies.append(copy)
    arrived[d] = outgoing[d]
    acc[...] = jnp.zeros_like(acc)
    for copy in copies:
        copy.wait()
    flat_ref[...] = jnp.concatenate([unfold(arrived[s]) for s in range(4)], 0).astype(bf16)

    def pair_copy(k):
        return send(
            pair_out.at[k], pair_in.at[k], pair_sems.at[0, k], pair_sems.at[1, k], {"tp": sibling}
        )

    def far_copy(k):
        return send(
            far_out.at[k], far_in.at[k], far_sems.at[0, k], far_sems.at[1, k], {"tp": far}
        )

    def hid_copy(k):
        return send(
            hid_own.at[k], hid_in.at[k], hid_sems.at[0, k], hid_sems.at[1, k], {"tp": sibling}
        )

    mine = pl.ds(pl.multiple_of(core * half, half), half)
    others = pl.ds(pl.multiple_of((1 - core) * half, half), half)

    @pl.loop(0, CHUNKS + 4)
    def _(s):
        @pl.when(s < CHUNKS)
        def _():
            k = s
            up_copy(k).wait()
            pair_out[k] = lax.dot_general(
                flat_ref[...], weights[k, others, :], NT, preferred_element_type=f32
            ).astype(bf16)
            pair_copy(k).start()
            own_pre[k] = lax.dot_general(
                flat_ref[...], weights[k, mine, :], NT, preferred_element_type=f32
            )

            @pl.when(k < 2 * CHUNKS - slots)
            def _():
                down_copy(k + slots - CHUNKS).start()

        @pl.when((s >= 1) & (s < CHUNKS + 1))
        def _():
            k = s - 1
            pair_copy(k).wait()
            both = own_pre[k] + pair_in[k].astype(f32)
            own_pre[k] = both
            far_out[k] = both.astype(bf16)
            far_copy(k).start()

        @pl.when((s >= 3) & (s < CHUNKS + 3))
        def _():
            k = s - 3
            far_copy(k).wait()
            pre = own_pre[k] + far_in[k].astype(f32)
            hid_own[k] = (pre / (1.0 + jnp.exp(-pre))).astype(bf16)
            hid_copy(k).start()

        @pl.when(s >= 4)
        def _():
            k = s - 4
            place_k = lax.rem(k + CHUNKS, slots)
            down_copy(k).wait()
            acc[...] += jnp.dot(
                hid_own[k], weights[place_k, mine, :], preferred_element_type=f32
            )
            hid_copy(k).wait()
            acc[...] += jnp.dot(
                hid_in[k], weights[place_k, others, :], preferred_element_type=f32
            )

    for s in range(4):
        back_out[s] = fold(acc[s * CAP : (s + 1) * CAP, :])
    copies = []
    for off in range(1, 4):
        peer = lax.rem(d + off, 4)
        copy = send(
            back_out.at[peer],
            back_in.at[d],
            back_sems.at[0, off],
            back_sems.at[1, off],
            {"dev": peer},
        )
        copy.start()
        copies.append(copy)
    back_in[d] = back_out[d]
    for copy in copies:
        copy.wait()
    returned = jnp.concatenate([unfold(back_in[s]) for s in range(4)], 0).astype(bf16)
    out_ref[...] = (
        mixed_ref[...]
        + first_gate * jnp.dot(pick_first, returned, preferred_element_type=f32)
        + second_gate * jnp.dot(pick_second, returned, preferred_element_type=f32)
    ).astype(bf16)


def fused_layer(
    attention, residual_input, norm_gain, router_weight, routes, out_weight, up_weight, down_weight
):
    row_count, features = residual_input.shape
    hidden = up_weight.shape[0]
    chunk = hidden // CHUNKS
    half = chunk // 2
    rows = 4 * CAP
    slots = 14
    f32, bf16 = jnp.float32, jnp.bfloat16
    vmem = pl.BlockSpec(memory_space=pltpu.VMEM)
    hbm = pl.BlockSpec(memory_space=pl.ANY)
    dma = pltpu.SemaphoreType.DMA
    folded = (4, 2 * CAP, features // 2)
    block = (row_count, features)
    cuts = 3
    piece = (row_count, features // cuts)
    scratch = [
        pltpu.VMEM((slots, chunk, features), bf16),
        pltpu.VMEM(out_weight.shape, bf16),
        pltpu.VMEM((4,) + block, bf16),
        pltpu.VMEM((cuts, 4) + piece, f32),
        pltpu.VMEM((cuts, 2) + piece, bf16),
        pltpu.VMEM((cuts, 2) + piece, bf16),
        pltpu.VMEM((cuts,) + piece, bf16),
        pltpu.VMEM((cuts,) + piece, bf16),
        pltpu.VMEM((cuts,) + piece, bf16),
        pltpu.VMEM((cuts,) + piece, bf16),
        pltpu.VMEM(block, f32),
        pltpu.VMEM((row_count, 128), f32),
        pltpu.VMEM((4, row_count, 128), f32),
        pltpu.VMEM(folded, bf16),
        pltpu.VMEM(folded, bf16),
        pltpu.VMEM((rows, features), bf16),
        pltpu.VMEM((CHUNKS, rows, half), bf16),
        pltpu.VMEM((CHUNKS, rows, half), bf16),
        pltpu.VMEM((CHUNKS, rows, half), f32),
        pltpu.VMEM((CHUNKS, rows, half), bf16),
        pltpu.VMEM((CHUNKS, rows, half), bf16),
        pltpu.VMEM((CHUNKS, rows, half), bf16),
        pltpu.VMEM((CHUNKS, rows, half), bf16),
        pltpu.VMEM((rows, features), f32),
        pltpu.VMEM(folded, bf16),
        pltpu.VMEM(folded, bf16),
        dma((2 * CHUNKS,)),
        dma,
        dma((2, 4)),
        dma((6, cuts)),
        dma((2, 4)),
        dma((2, 4)),
        dma((2, 4)),
        dma((2, CHUNKS)),
        dma((2, CHUNKS)),
        dma((2, CHUNKS)),
    ]
    return pl.pallas_call(
        layer_kernel,
        out_shape=jax.ShapeDtypeStruct(block, bf16),
        in_specs=[vmem] * 5 + [hbm] * 3,
        out_specs=vmem,
        scratch_shapes=scratch,
        compiler_params=pltpu.CompilerParams(
            collective_id=0, has_side_effects=True, vmem_limit_bytes=60 * 1024 * 1024
        ),
        cost_estimate=pl.CostEstimate(
            flops=4 * rows * hidden * features,
            bytes_accessed=4 * hidden * features + out_weight.size * 2,
            transcendentals=rows * hidden,
        ),
    )(
        attention,
        residual_input,
        norm_gain.reshape(features // 128, 128),
        router_weight.T,
        routes.T,
        out_weight,
        up_weight,
        down_weight,
    )


def sum_heads(terms):
    return lax.psum_scatter(terms, "tp", scatter_dimension=1, tiled=True)


def body(
    residual_input,
    queries,
    new_kv,
    cache,
    lengths,
    slots,
    out_weight,
    norm_gain,
    router_weight,
    up_weight,
    down_weight,
    routes,
):
    row_count = residual_input.shape[0]
    features = residual_input.shape[1]
    kv_local = cache.shape[3] // HEAD_DIM
    group = queries.shape[1] // cache.shape[3]
    positions = cache.shape[2]
    experts = router_weight.shape[1]
    devices = lax.axis_size("dev")
    pieces = devices // experts
    capacity = CAP
    placing = (slots[:, None] == lax.broadcasted_iota(jnp.int32, (row_count, row_count), 1)).astype(
        jnp.bfloat16
    )
    contract_rows = (((0,), (0,)), ((), ()))
    query_slot = lax.dot_general(
        placing, queries, contract_rows, preferred_element_type=jnp.float32
    ).astype(jnp.bfloat16)
    current_slot = lax.dot_general(
        placing, new_kv.reshape(row_count, -1), contract_rows, preferred_element_type=jnp.float32
    ).astype(jnp.bfloat16)
    current_slot = current_slot.reshape(row_count, 2, kv_local, HEAD_DIM)
    query_vector = query_slot.reshape(row_count, kv_local, group, HEAD_DIM)
    keys = cache[:, 0].reshape(row_count, positions, kv_local, HEAD_DIM)
    values = cache[:, 1].reshape(row_count, positions, kv_local, HEAD_DIM)
    scale = HEAD_DIM ** (-0.5)
    scores = (
        jnp.einsum("bkgd,blkd->bkgl", query_vector, keys, preferred_element_type=jnp.float32)
        * scale
    )
    own = (
        jnp.einsum(
            "orwm,orm->orw", query_vector, current_slot[:, 0], preferred_element_type=jnp.float32
        )
        * scale
    )
    mask = lax.broadcasted_iota(jnp.int32, (1, 1, 1, positions), 3) < lengths[:, None, None, None]
    scores = jnp.where(mask, scores, -jnp.inf)
    top = jnp.maximum(jnp.max(scores, -1), own)
    raised = jnp.exp(scores - top[..., None])
    own_raised = jnp.exp(own - top)
    total = jnp.sum(raised, -1) + own_raised
    probs = (raised / total[..., None]).astype(jnp.bfloat16)
    own_prob = (own_raised / total).astype(jnp.bfloat16)
    attended = jnp.einsum("bkgl,blkd->bkgd", probs, values, preferred_element_type=jnp.float32)
    attended = (
        attended
        + own_prob.astype(jnp.float32)[..., None]
        * current_slot[:, 1].astype(jnp.float32)[:, :, None, :]
    )
    attention_slot = attended.reshape(row_count, -1).astype(jnp.bfloat16)
    attention = jnp.dot(placing, attention_slot, preferred_element_type=jnp.float32).astype(
        jnp.bfloat16
    )
    if devices == 4 and lax.axis_size("tp") == 4 and experts == 4:
        return fused_layer(
            attention,
            residual_input,
            norm_gain,
            router_weight,
            routes,
            out_weight,
            up_weight,
            down_weight,
        )
    partial_rows = jnp.dot(
        lax.all_gather(attention, "dev", axis=0, tiled=True),
        out_weight,
        preferred_element_type=jnp.float32,
    )
    terms = lax.all_to_all(partial_rows, "dev", split_axis=0, concat_axis=1, tiled=True)
    projected = sum_heads(terms)
    mixed = residual_input.astype(jnp.float32) + projected
    gained = mixed * norm_gain
    router = router_weight.astype(jnp.float32)
    square = lax.psum(jnp.sum(mixed * mixed, 1), "tp")
    scale_row = lax.rsqrt(square / D + eps)
    normed_wide = gained * scale_row[:, None]
    logits = lax.psum(jnp.dot(normed_wide, router, precision=lax.Precision.HIGHEST), "tp")
    normed = normed_wide.astype(jnp.bfloat16)
    expert_ids = lax.broadcasted_iota(jnp.int32, (row_count, experts), 1)
    first = (routes[:, 0:1] == expert_ids).astype(jnp.float32)
    second = (routes[:, 1:2] == expert_ids).astype(jnp.float32)
    first_logit = jnp.sum(logits * first, 1)
    second_logit = jnp.sum(logits * second, 1)
    first_gate = 1.0 / (1.0 + jnp.exp(second_logit - first_logit))
    second_gate = 1.0 / (1.0 + jnp.exp(first_logit - second_logit))
    row_weight_matrix = first * first_gate[:, None] + second * second_gate[:, None]
    member = first + second
    position = jnp.cumsum(member, 0) - member
    slot_grid = lax.broadcasted_iota(jnp.float32, (1, capacity, 1), 1)
    selection = member.T[:, None, :] * (position.T[:, None, :] == slot_grid).astype(jnp.float32)
    outgoing = jnp.einsum(
        "ecb,bf->ecf", selection.astype(jnp.bfloat16), normed, preferred_element_type=jnp.float32
    ).astype(jnp.bfloat16)
    outgoing = jnp.broadcast_to(outgoing[:, None], (experts, pieces, capacity, features)).reshape(
        devices, capacity, features
    )
    arrived = lax.all_to_all(outgoing, "dev", split_axis=0, concat_axis=0, tiled=True)
    count = arrived.shape[1]
    flat = arrived.reshape(devices * count, features)
    pre = lax.dot_general(
        flat, up_weight, (((1,), (1,)), ((), ())), preferred_element_type=jnp.float32
    )
    summed = lax.psum(pre, "tp")
    hidden = jax.nn.silu(summed).astype(jnp.bfloat16)
    part = jnp.dot(hidden, down_weight, preferred_element_type=jnp.float32).astype(jnp.bfloat16)
    returned = lax.all_to_all(
        part.reshape(devices, count, features), "dev", split_axis=0, concat_axis=0, tiled=True
    )
    expert_sum = jnp.sum(
        returned.reshape(experts, pieces, capacity, features).astype(jnp.float32), 1
    )
    placed = selection * row_weight_matrix.T[:, None, :]
    moe = jnp.einsum("ecb,ecf->bf", placed, expert_sum, precision=lax.Precision.HIGHEST)
    return (mixed + moe).astype(jnp.bfloat16)


def solution(mesh):
    in_specs = (
        P(("grp", "dev"), "tp"),
        P(("grp", "dev"), "tp"),
        P(("grp", "dev"), None, "tp"),
        P(("grp", "dev"), None, None, "tp"),
        P(("grp", "dev")),
        P(("grp", "dev")),
        P("tp", "dev"),
        P("tp"),
        P("tp", None),
        P("dev", "tp"),
        P("dev", "tp"),
        P(("grp", "dev"), None),
    )
    out_specs = P(("grp", "dev"), "tp")
    return jax.shard_map(body, mesh=mesh, in_specs=in_specs, out_specs=out_specs, check_vma=False)
```

```python
import jax
import jax.numpy as jnp
from jax import lax
from jax.experimental import pallas as pl
from jax.experimental.pallas import tpu as pltpu
from jax.sharding import PartitionSpec as P

D = 6144
HEAD_DIM = 128
CAP = 24


eps = 1e-05


MESH = pl.DeviceIdType.MESH
CHUNKS = 8
NT = (((1,), (1,)), ((), ()))


def send(source, target, send_sem, recv_sem, where):
    return pltpu.make_async_remote_copy(
        src_ref=source,
        dst_ref=target,
        send_sem=send_sem,
        recv_sem=recv_sem,
        device_id=where,
        device_id_type=MESH,
    )


def fold(block):
    half = block.shape[1] // 2
    return jnp.concatenate([block[:, :half], block[:, half:]], 0).astype(jnp.bfloat16)


def unfold(block):
    rows = block.shape[0] // 2
    wide = block.astype(jnp.float32)
    return jnp.concatenate([wide[:rows], wide[rows:]], 1)


def layer_kernel(
    slots_ref,
    att_slot_ref,
    res_ref,
    gain_ref,
    router_ref,
    routes_t_ref,
    outw_hbm,
    up_hbm,
    down_hbm,
    out_ref,
    weights,
    outw,
    att_ref,
    gathered,
    projected,
    core_out,
    core_in,
    x_out,
    x_in,
    turn_out,
    turn_in,
    mixed_ref,
    stat_out,
    stat_in,
    outgoing,
    arrived,
    flat_ref,
    pair_out,
    pair_in,
    own_pre,
    far_out,
    far_in,
    hid_own,
    hid_in,
    acc,
    back_out,
    back_in,
    weight_sem,
    outw_sem,
    gather_sems,
    hop_sems,
    stat_sems,
    there_sems,
    back_sems,
    pair_sems,
    far_sems,
    hid_sems,
):
    devices, row_count, features = gathered.shape
    slots = weights.shape[0]
    chunk = weights.shape[1]
    half = chunk // 2
    experts = router_ref.shape[0]
    f32 = jnp.float32
    bf16 = jnp.bfloat16
    d = lax.axis_index("dev")
    t = lax.axis_index("tp")
    core = lax.rem(t, 2)
    x = t // 2
    sibling = x * 2 + (1 - core)
    far = (1 - x) * 2 + core

    def up_copy(k):
        return pltpu.make_async_copy(
            up_hbm.at[pl.ds(k * chunk, chunk)], weights.at[k], weight_sem.at[k]
        )

    def down_copy(k):
        return pltpu.make_async_copy(
            down_hbm.at[pl.ds(k * chunk, chunk)],
            weights.at[lax.rem(k + CHUNKS, slots)],
            weight_sem.at[k + CHUNKS],
        )

    outw_copy = pltpu.make_async_copy(outw_hbm, outw, outw_sem)
    outw_copy.start()
    for k in range(CHUNKS):
        up_copy(k).start()
    for k in range(slots - CHUNKS):
        down_copy(k).start()

    barrier = pltpu.get_barrier_semaphore()
    for off in range(1, 4):
        pl.semaphore_signal(
            barrier, inc=1, device_id={"dev": lax.rem(d + off, 4)}, device_id_type=MESH
        )
        pl.semaphore_signal(
            barrier, inc=1, device_id={"tp": lax.rem(t + off, 4)}, device_id_type=MESH
        )

    @pl.when(d != t)
    def _():
        pl.semaphore_signal(barrier, inc=1, device_id={"dev": t, "tp": d}, device_id_type=MESH)

    row_i = lax.broadcasted_iota(jnp.int32, (row_count, row_count), 0)
    row_j = lax.broadcasted_iota(jnp.int32, (row_count, row_count), 1)
    same = row_i == row_j
    row_slot = jnp.sum(
        jnp.where(same, slots_ref[...].astype(f32), 0.0), 1, keepdims=True
    )
    placing = (row_j.astype(f32) == row_slot).astype(bf16)
    placed = jnp.dot(placing, att_slot_ref[...], preferred_element_type=f32).astype(bf16)
    att_ref[...] = placed
    gathered[d] = placed

    @pl.when(d != t)
    def _():
        pl.semaphore_wait(barrier, 7)

    @pl.when(d == t)
    def _():
        pl.semaphore_wait(barrier, 6)

    copies = []
    for off in range(1, 4):
        copy = send(
            att_ref,
            gathered.at[d],
            gather_sems.at[0, off],
            gather_sems.at[1, off],
            {"dev": lax.rem(d + off, 4)},
        )
        copy.start()
        copies.append(copy)
    outw_copy.wait()
    for copy in copies:
        copy.wait()

    rows_all = gathered[...].reshape(devices * row_count, features)

    cuts = core_out.shape[0]
    width = features // cuts
    core_copies = []
    for j in range(cuts):
        cols = slice(j * width, (j + 1) * width)
        projected[j] = jnp.dot(
            rows_all, outw[:, cols], preferred_element_type=f32
        ).reshape(devices, row_count, width)
        core_out[j, 0] = projected[j, 1 - core].astype(bf16)
        core_out[j, 1] = projected[j, 3 - core].astype(bf16)
        copy = send(
            core_out.at[j], core_in.at[j], hop_sems.at[0, j], hop_sems.at[1, j], {"tp": sibling}
        )
        copy.start()
        core_copies.append(copy)
    x_copies = []
    for j in range(cuts):
        core_copies[j].wait()
        x_out[j] = (projected[j, far] + core_in[j, 1 - x].astype(f32)).astype(bf16)
        copy = send(x_out.at[j], x_in.at[j], hop_sems.at[2, j], hop_sems.at[3, j], {"tp": far})
        copy.start()
        x_copies.append(copy)

    def turn_copy(j):
        return send(
            turn_out.at[j],
            turn_in.at[j],
            hop_sems.at[4, j],
            hop_sems.at[5, j],
            {"dev": t, "tp": d},
        )

    for j in range(cuts):
        x_copies[j].wait()
        turn_out[j] = (
            projected[j, t] + core_in[j, x].astype(f32) + x_in[j].astype(f32)
        ).astype(bf16)

        @pl.when(d != t)
        def _():
            turn_copy(j).start()

        @pl.when(d == t)
        def _():
            turn_in[j] = turn_out[j]

    @pl.when(d != t)
    def _():
        for j in range(cuts):
            turn_copy(j).wait()

    turned = jnp.concatenate([turn_in[j] for j in range(cuts)], 1)
    mixed = res_ref[...].astype(f32) + turned.astype(f32)
    mixed_ref[...] = mixed
    gain = jnp.concatenate([gain_ref[i : i + 1, :] for i in range(gain_ref.shape[0])], 1)
    gained = mixed * gain
    lane = lax.broadcasted_iota(jnp.int32, (row_count, 128), 1)
    stat = jnp.where(lane == experts, jnp.sum(mixed * mixed, 1, keepdims=True), 0.0)
    router = router_ref[...].astype(f32)
    for e in range(experts):
        stat = jnp.where(
            lane == e, jnp.sum(gained * router[e : e + 1, :], 1, keepdims=True), stat
        )
    stat_out[...] = stat
    copies = []
    for off in range(1, 4):
        copy = send(
            stat_out,
            stat_in.at[off],
            stat_sems.at[0, off],
            stat_sems.at[1, off],
            {"tp": lax.rem(t + off, 4)},
        )
        copy.start()
        copies.append(copy)

    routes_wide = routes_t_ref[...].astype(f32)
    first = jnp.sum(jnp.where(same, routes_wide[0:1, :], 0.0), 1, keepdims=True)
    second = jnp.sum(jnp.where(same, routes_wide[1:2, :], 0.0), 1, keepdims=True)
    first_hot = (lane.astype(f32) == first).astype(f32)
    second_hot = (lane.astype(f32) == second).astype(f32)
    place = jnp.dot(
        (row_j < row_i).astype(bf16),
        (first_hot + second_hot).astype(bf16),
        preferred_element_type=f32,
    )
    first_place = jnp.sum(first_hot * place, 1, keepdims=True)
    second_place = jnp.sum(second_hot * place, 1, keepdims=True)
    wide_lane = lax.broadcasted_iota(jnp.int32, (row_count, experts * CAP), 1)
    pick_first = (
        wide_lane.astype(f32) == first * CAP + first_place
    ).astype(bf16)
    pick_second = (
        wide_lane.astype(f32) == second * CAP + second_place
    ).astype(bf16)
    across = lax.broadcasted_iota(jnp.int32, (8, row_count), 0)
    member_t = (across == routes_t_ref[0:1, :]).astype(f32) + (
        across == routes_t_ref[1:2, :]
    ).astype(f32)
    place_t = jnp.dot(
        member_t.astype(bf16), (row_i < row_j).astype(bf16), preferred_element_type=f32
    )
    slot = lax.broadcasted_iota(jnp.int32, (CAP, row_count), 0).astype(f32)
    select = jnp.concatenate(
        [
            jnp.where(slot == place_t[e : e + 1, :], member_t[e : e + 1, :], 0.0)
            for e in range(experts)
        ],
        0,
    ).astype(bf16)

    for copy in copies:
        copy.wait()
    stat = stat + stat_in[1] + stat_in[2] + stat_in[3]
    square = jnp.sum(jnp.where(lane == experts, stat, 0.0), 1, keepdims=True)
    scale_row = lax.rsqrt(square / D + eps)
    logits = stat * scale_row
    first_logit = jnp.sum(first_hot * logits, 1, keepdims=True)
    second_logit = jnp.sum(second_hot * logits, 1, keepdims=True)
    first_gate = 1.0 / (1.0 + jnp.exp(second_logit - first_logit))
    second_gate = 1.0 / (1.0 + jnp.exp(first_logit - second_logit))
    normed = (gained * scale_row).astype(bf16)
    picked = jnp.dot(select, normed, preferred_element_type=f32)
    for e in range(experts):
        outgoing[e] = fold(picked[e * CAP : (e + 1) * CAP])
    copies = []
    for off in range(1, 4):
        peer = lax.rem(d + off, 4)
        copy = send(
            outgoing.at[peer],
            arrived.at[d],
            there_sems.at[0, off],
            there_sems.at[1, off],
            {"dev": peer},
        )
        copy.start()
        copies.append(copy)
    arrived[d] = outgoing[d]
    acc[...] = jnp.zeros_like(acc)
    for copy in copies:
        copy.wait()
    flat_ref[...] = jnp.concatenate([unfold(arrived[s]) for s in range(4)], 0).astype(bf16)

    def pair_copy(k):
        return send(
            pair_out.at[k], pair_in.at[k], pair_sems.at[0, k], pair_sems.at[1, k], {"tp": sibling}
        )

    def far_copy(k):
        return send(
            far_out.at[k], far_in.at[k], far_sems.at[0, k], far_sems.at[1, k], {"tp": far}
        )

    def hid_copy(k):
        return send(
            hid_own.at[k], hid_in.at[k], hid_sems.at[0, k], hid_sems.at[1, k], {"tp": sibling}
        )

    mine = pl.ds(pl.multiple_of(core * half, half), half)
    others = pl.ds(pl.multiple_of((1 - core) * half, half), half)

    @pl.loop(0, CHUNKS + 4)
    def _(s):
        @pl.when((s >= 1) & (s < CHUNKS + 1))
        def _():
            k = s - 1
            pair_copy(k).wait()
            both = own_pre[k] + pair_in[k].astype(f32)
            own_pre[k] = both
            far_out[k] = both.astype(bf16)
            far_copy(k).start()

        @pl.when(s < CHUNKS)
        def _():
            k = s
            up_copy(k).wait()
            pair_out[k] = lax.dot_general(
                flat_ref[...], weights[k, others, :], NT, preferred_element_type=f32
            ).astype(bf16)
            pair_copy(k).start()
            own_pre[k] = lax.dot_general(
                flat_ref[...], weights[k, mine, :], NT, preferred_element_type=f32
            )

            @pl.when(k < 2 * CHUNKS - slots)
            def _():
                down_copy(k + slots - CHUNKS).start()

        @pl.when((s >= 3) & (s < CHUNKS + 3))
        def _():
            k = s - 3
            far_copy(k).wait()
            pre = own_pre[k] + far_in[k].astype(f32)
            hid_own[k] = (pre / (1.0 + jnp.exp(-pre))).astype(bf16)
            hid_copy(k).start()

        @pl.when(s >= 4)
        def _():
            k = s - 4
            place_k = lax.rem(k + CHUNKS, slots)
            down_copy(k).wait()
            acc[...] += jnp.dot(
                hid_own[k], weights[place_k, mine, :], preferred_element_type=f32
            )
            hid_copy(k).wait()
            acc[...] += jnp.dot(
                hid_in[k], weights[place_k, others, :], preferred_element_type=f32
            )

    for s in range(4):
        back_out[s] = fold(acc[s * CAP : (s + 1) * CAP, :])
    copies = []
    for off in range(1, 4):
        peer = lax.rem(d + off, 4)
        copy = send(
            back_out.at[peer],
            back_in.at[d],
            back_sems.at[0, off],
            back_sems.at[1, off],
            {"dev": peer},
        )
        copy.start()
        copies.append(copy)
    back_in[d] = back_out[d]
    for copy in copies:
        copy.wait()
    returned = jnp.concatenate([unfold(back_in[s]) for s in range(4)], 0).astype(bf16)
    out_ref[...] = (
        mixed_ref[...]
        + first_gate * jnp.dot(pick_first, returned, preferred_element_type=f32)
        + second_gate * jnp.dot(pick_second, returned, preferred_element_type=f32)
    ).astype(bf16)


def fused_layer(
    slot_of, attention, residual_input, norm_gain, router_weight, routes, out_weight, up_weight, down_weight
):
    row_count, features = residual_input.shape
    hidden = up_weight.shape[0]
    chunk = hidden // CHUNKS
    half = chunk // 2
    rows = 4 * CAP
    slots = 14
    f32, bf16 = jnp.float32, jnp.bfloat16
    vmem = pl.BlockSpec(memory_space=pltpu.VMEM)
    hbm = pl.BlockSpec(memory_space=pl.ANY)
    dma = pltpu.SemaphoreType.DMA
    folded = (4, 2 * CAP, features // 2)
    block = (row_count, features)
    cuts = 3
    piece = (row_count, features // cuts)
    scratch = [
        pltpu.VMEM((slots, chunk, features), bf16),
        pltpu.VMEM(out_weight.shape, bf16),
        pltpu.VMEM(block, bf16),
        pltpu.VMEM((4,) + block, bf16),
        pltpu.VMEM((cuts, 4) + piece, f32),
        pltpu.VMEM((cuts, 2) + piece, bf16),
        pltpu.VMEM((cuts, 2) + piece, bf16),
        pltpu.VMEM((cuts,) + piece, bf16),
        pltpu.VMEM((cuts,) + piece, bf16),
        pltpu.VMEM((cuts,) + piece, bf16),
        pltpu.VMEM((cuts,) + piece, bf16),
        pltpu.VMEM(block, f32),
        pltpu.VMEM((row_count, 128), f32),
        pltpu.VMEM((4, row_count, 128), f32),
        pltpu.VMEM(folded, bf16),
        pltpu.VMEM(folded, bf16),
        pltpu.VMEM((rows, features), bf16),
        pltpu.VMEM((CHUNKS, rows, half), bf16),
        pltpu.VMEM((CHUNKS, rows, half), bf16),
        pltpu.VMEM((CHUNKS, rows, half), f32),
        pltpu.VMEM((CHUNKS, rows, half), bf16),
        pltpu.VMEM((CHUNKS, rows, half), bf16),
        pltpu.VMEM((CHUNKS, rows, half), bf16),
        pltpu.VMEM((CHUNKS, rows, half), bf16),
        pltpu.VMEM((rows, features), f32),
        pltpu.VMEM(folded, bf16),
        pltpu.VMEM(folded, bf16),
        dma((2 * CHUNKS,)),
        dma,
        dma((2, 4)),
        dma((6, cuts)),
        dma((2, 4)),
        dma((2, 4)),
        dma((2, 4)),
        dma((2, CHUNKS)),
        dma((2, CHUNKS)),
        dma((2, CHUNKS)),
    ]
    return pl.pallas_call(
        layer_kernel,
        out_shape=jax.ShapeDtypeStruct(block, bf16),
        in_specs=[vmem] * 6 + [hbm] * 3,
        out_specs=vmem,
        scratch_shapes=scratch,
        compiler_params=pltpu.CompilerParams(
            collective_id=0, has_side_effects=True, vmem_limit_bytes=60 * 1024 * 1024
        ),
        cost_estimate=pl.CostEstimate(
            flops=4 * rows * hidden * features,
            bytes_accessed=4 * hidden * features + out_weight.size * 2,
            transcendentals=rows * hidden,
        ),
    )(
        slot_of.reshape(1, row_count),
        attention,
        residual_input,
        norm_gain.reshape(features // 128, 128),
        router_weight.T,
        routes.T,
        out_weight,
        up_weight,
        down_weight,
    )


def sum_heads(terms):
    return lax.psum_scatter(terms, "tp", scatter_dimension=1, tiled=True)


def body(
    residual_input,
    queries,
    new_kv,
    cache,
    lengths,
    slots,
    out_weight,
    norm_gain,
    router_weight,
    up_weight,
    down_weight,
    routes,
):
    row_count = residual_input.shape[0]
    features = residual_input.shape[1]
    kv_local = cache.shape[3] // HEAD_DIM
    group = queries.shape[1] // cache.shape[3]
    positions = cache.shape[2]
    experts = router_weight.shape[1]
    devices = lax.axis_size("dev")
    pieces = devices // experts
    capacity = CAP
    placing = (slots[:, None] == lax.broadcasted_iota(jnp.int32, (row_count, row_count), 1)).astype(
        jnp.bfloat16
    )
    contract_rows = (((0,), (0,)), ((), ()))
    query_slot = lax.dot_general(
        placing, queries, contract_rows, preferred_element_type=jnp.float32
    ).astype(jnp.bfloat16)
    current_slot = lax.dot_general(
        placing, new_kv.reshape(row_count, -1), contract_rows, preferred_element_type=jnp.float32
    ).astype(jnp.bfloat16)
    current_slot = current_slot.reshape(row_count, 2, kv_local, HEAD_DIM)
    query_vector = query_slot.reshape(row_count, kv_local, group, HEAD_DIM)
    keys = cache[:, 0].reshape(row_count, positions, kv_local, HEAD_DIM)
    values = cache[:, 1].reshape(row_count, positions, kv_local, HEAD_DIM)
    scale = HEAD_DIM ** (-0.5)
    scores = (
        jnp.einsum("bkgd,blkd->bkgl", query_vector, keys, preferred_element_type=jnp.float32)
        * scale
    )
    own = (
        jnp.einsum(
            "orwm,orm->orw", query_vector, current_slot[:, 0], preferred_element_type=jnp.float32
        )
        * scale
    )
    mask = lax.broadcasted_iota(jnp.int32, (1, 1, 1, positions), 3) < lengths[:, None, None, None]
    scores = jnp.where(mask, scores, -jnp.inf)
    top = jnp.maximum(jnp.max(scores, -1), own)
    raised = jnp.exp(scores - top[..., None])
    own_raised = jnp.exp(own - top)
    total = jnp.sum(raised, -1) + own_raised
    probs = (raised / total[..., None]).astype(jnp.bfloat16)
    own_prob = (own_raised / total).astype(jnp.bfloat16)
    attended = jnp.einsum("bkgl,blkd->bkgd", probs, values, preferred_element_type=jnp.float32)
    attended = (
        attended
        + own_prob.astype(jnp.float32)[..., None]
        * current_slot[:, 1].astype(jnp.float32)[:, :, None, :]
    )
    attention_slot = attended.reshape(row_count, -1).astype(jnp.bfloat16)
    if devices == 4 and lax.axis_size("tp") == 4 and experts == 4:
        return fused_layer(
            slots,
            attention_slot,
            residual_input,
            norm_gain,
            router_weight,
            routes,
            out_weight,
            up_weight,
            down_weight,
        )
    attention = jnp.dot(placing, attention_slot, preferred_element_type=jnp.float32).astype(
        jnp.bfloat16
    )
    partial_rows = jnp.dot(
        lax.all_gather(attention, "dev", axis=0, tiled=True),
        out_weight,
        preferred_element_type=jnp.float32,
    )
    terms = lax.all_to_all(partial_rows, "dev", split_axis=0, concat_axis=1, tiled=True)
    projected = sum_heads(terms)
    mixed = residual_input.astype(jnp.float32) + projected
    gained = mixed * norm_gain
    router = router_weight.astype(jnp.float32)
    square = lax.psum(jnp.sum(mixed * mixed, 1), "tp")
    scale_row = lax.rsqrt(square / D + eps)
    normed_wide = gained * scale_row[:, None]
    logits = lax.psum(jnp.dot(normed_wide, router, precision=lax.Precision.HIGHEST), "tp")
    normed = normed_wide.astype(jnp.bfloat16)
    expert_ids = lax.broadcasted_iota(jnp.int32, (row_count, experts), 1)
    first = (routes[:, 0:1] == expert_ids).astype(jnp.float32)
    second = (routes[:, 1:2] == expert_ids).astype(jnp.float32)
    first_logit = jnp.sum(logits * first, 1)
    second_logit = jnp.sum(logits * second, 1)
    first_gate = 1.0 / (1.0 + jnp.exp(second_logit - first_logit))
    second_gate = 1.0 / (1.0 + jnp.exp(first_logit - second_logit))
    row_weight_matrix = first * first_gate[:, None] + second * second_gate[:, None]
    member = first + second
    position = jnp.cumsum(member, 0) - member
    slot_grid = lax.broadcasted_iota(jnp.float32, (1, capacity, 1), 1)
    selection = member.T[:, None, :] * (position.T[:, None, :] == slot_grid).astype(jnp.float32)
    outgoing = jnp.einsum(
        "ecb,bf->ecf", selection.astype(jnp.bfloat16), normed, preferred_element_type=jnp.float32
    ).astype(jnp.bfloat16)
    outgoing = jnp.broadcast_to(outgoing[:, None], (experts, pieces, capacity, features)).reshape(
        devices, capacity, features
    )
    arrived = lax.all_to_all(outgoing, "dev", split_axis=0, concat_axis=0, tiled=True)
    count = arrived.shape[1]
    flat = arrived.reshape(devices * count, features)
    pre = lax.dot_general(
        flat, up_weight, (((1,), (1,)), ((), ())), preferred_element_type=jnp.float32
    )
    summed = lax.psum(pre, "tp")
    hidden = jax.nn.silu(summed).astype(jnp.bfloat16)
    part = jnp.dot(hidden, down_weight, preferred_element_type=jnp.float32).astype(jnp.bfloat16)
    returned = lax.all_to_all(
        part.reshape(devices, count, features), "dev", split_axis=0, concat_axis=0, tiled=True
    )
    expert_sum = jnp.sum(
        returned.reshape(experts, pieces, capacity, features).astype(jnp.float32), 1
    )
    placed = selection * row_weight_matrix.T[:, None, :]
    moe = jnp.einsum("ecb,ecf->bf", placed, expert_sum, precision=lax.Precision.HIGHEST)
    return (mixed + moe).astype(jnp.bfloat16)


def solution(mesh):
    in_specs = (
        P(("grp", "dev"), "tp"),
        P(("grp", "dev"), "tp"),
        P(("grp", "dev"), None, "tp"),
        P(("grp", "dev"), None, None, "tp"),
        P(("grp", "dev")),
        P(("grp", "dev")),
        P("tp", "dev"),
        P("tp"),
        P("tp", None),
        P("dev", "tp"),
        P("dev", "tp"),
        P(("grp", "dev"), None),
    )
    out_specs = P(("grp", "dev"), "tp")
    return jax.shard_map(body, mesh=mesh, in_specs=in_specs, out_specs=out_specs, check_vma=False)
```
